256 devices in a mesh: cfg: 2 (over y_lo), req: 8 (over x, core), seq: 16 (over z, y_hi).
Axes of the slice: x: 4, y: 4 (y_hi: 2, y_lo: 2; y = y_hi * 2 + y_lo), z: 8, core: 2. Of those that a mesh axis runs over, the one named last changes fastest.
Arguments:
- image_hidden: bfloat16 [2, 8, 2048, 1536], P('cfg', 'req', 'seq'), may hold values from -6 to 6
- text_hidden: bfloat16 [2, 8, 160, 1536], P('cfg', 'req', 'seq'), may hold values from -6 to 6
- modulation: float32 [2, 8, 10, 1536], P('cfg', 'req'), may hold values from -3 to 3
- attn_weight: bfloat16 [1536, 5120], P(None, 'seq'), may hold values from -8 to 8
- proj_weight: bfloat16 [1024, 1536], replicated, may hold values from -0.1875 to 0.1875
- mlp_in_weight: bfloat16 [1536, 6144], P(None, 'seq'), may hold values from -0.15625 to 0.15625
- mlp_out_weight: bfloat16 [6144, 1536], P('seq'), may hold values from -0.078125 to 0.078125
- final_weight: bfloat16 [64, 1536], replicated, may hold values from -0.15625 to 0.15625
- latents: float32 [8, 64, 2048], P('req', 'cfg', 'seq'), may hold values from -6 to 6
- guidance: float32 [8], P('req'), may hold values from 3 to 7
- text_lengths: int32 [2, 8], P('cfg', 'req'), may hold values from 1 to 154, 693 in all within a row
- step_index: int32 [8], P('req'), may hold values from 0 to 27
- step_count: int32 [8], P('req'), may hold values from 1 to 3
Outputs:
- velocity: float32 [8, 64, 2048], P('req', 'cfg', 'seq')
- new_latents: float32 [8, 64, 2048], P('req', 'cfg', 'seq')
The draws below stay inside these ranges and needn't reach their ends.
All inputs are finite; a program needn't handle non-finite values. No bound on the sum of `text_lengths` on one device may be relied on, other than what follows from the above.
Results may differ from the reference program's by a relative error of at most 0.017.
Values may be sent and summed in bfloat16 or wider, within the bound.
No kernel may reach another device: no remote copies, remote signals or barrier semaphores. Data moves between devices by JAX's collectives and lax.ppermute only.
A program may use at most 128 MiB of HBM per device.

```python
import math
import jax
import jax.numpy as jnp
import numpy as np
from jax import lax

D = 1536
HEADS = 16
HEAD = 64
FF = 6144
PATCH = 64
TXT = 160
TXT_MAX = 154
STEPS = 28
IMG = 2048
REQ = 8
N_SEQ = 16


def draw_attn_weight(key, part):
    base = jnp.clip(jax.random.normal(key, (D, HEADS, 5, HEAD), jnp.float32), -6.0, 6.0) / jnp.sqrt(float(D))
    base = jnp.clip(base, -8.0, 8.0)
    return base.reshape(D, HEADS * 5 * HEAD).astype(jnp.bfloat16)


def draw_image_hidden(key, part):
    first_key = jax.random.fold_in(key, 21)
    second_key = jax.random.fold_in(key, 22)
    ramp = (jnp.arange(IMG, dtype=jnp.float32) + 0.5) / IMG
    shared = jnp.clip(jax.random.normal(first_key, (REQ, IMG, D), jnp.float32), -6.0, 6.0)
    other = jnp.clip(jax.random.normal(second_key, (REQ, IMG, D), jnp.float32), -6.0, 6.0)
    mixing = ramp[None, :, None]
    second = (1.0 - mixing) * shared + mixing * other
    result = jnp.clip(jnp.stack([shared, second], axis=0), -6.0, 6.0)
    return result.astype(jnp.bfloat16)


def draw_modulation(key, part):
    base = 0.5 * jax.random.normal(jax.random.fold_in(key, 31), (REQ, 10, D), jnp.float32)
    offset = 0.1 * jax.random.normal(jax.random.fold_in(key, 32), (REQ, 10, D), jnp.float32)
    result = jnp.stack([base, base + offset], axis=0)
    return jnp.clip(result, -3.0, 3.0).astype(jnp.float32)


def plant(array, own_key, smallest, top_value):
    longest = array.shape.index(max(array.shape))
    spots = []
    for shift in (0, 1):
        where = [jax.random.randint(jax.random.fold_in(own_key, axis), (), 0, length) for axis, length in enumerate(array.shape)]
        where[longest] = (where[longest] + shift) % array.shape[longest]
        spots.append(tuple(where))
    return array.at[spots[0]].set(smallest).at[spots[1]].set(top_value)


def levels(own_key, dims, shards, least, largest):
    gain, own = 1.0, jax.random.fold_in(own_key, 6)
    for axis_at, shards_of in shards:
        heights = jnp.exp(jax.random.uniform(jax.random.fold_in(own, axis_at), (shards_of,), jnp.float32, least / len(shards), largest / len(shards)))
        gain = gain * jnp.repeat(heights, dims[axis_at] // shards_of).reshape([-1 if axis == axis_at else 1 for axis in range(len(dims))])
    return gain


def split_up(number_of, total, most, lean):
    weights = [(1 << 20) // math.isqrt(rank ** lean) + 1 for rank in range(2, number_of + 1)]
    surplus, holding = total - most - (number_of - 1), [1] * (number_of - 1)
    while surplus > 0:
        movable = [i for i in range(number_of - 1) if holding[i] < most]
        whole, budget = sum([weights[i] for i in movable]), surplus
        for i in movable:
            extra = min(most - holding[i], max(1, budget * weights[i] // whole), surplus)
            holding[i] = holding[i] + extra
            surplus = surplus - extra
    return np.array([most] + holding)


def ragged_sizes(stream_key, count, total, most, slope):
    if count == 2:
        one = jax.random.randint(stream_key, (), max(1, total - most), min(most, total - 1) + 1)
        return jnp.stack([one, total - one])
    sizes = jnp.asarray(split_up(count, total, most, slope), jnp.int32)
    twos = (count - 1) // 2
    giver, sink = sizes[1:1 + 2 * twos:2], sizes[2:2 + 2 * twos:2]
    room = jnp.minimum(giver - 1, most - sink)
    passed = jax.random.randint(jax.random.fold_in(stream_key, 1), (twos,), 0, 1 << 20) % (room + 1)
    sizes = sizes.at[1:1 + 2 * twos:2].set(giver - passed).at[2:2 + 2 * twos:2].set(sink + passed)
    return sizes[jax.random.permutation(jax.random.fold_in(stream_key, 2), count)]


def normal_values(rng, shape, scale, reach, shards=(), held_as=jnp.bfloat16):
    level = levels(rng, shape, shards, -0.22, 0.18) if shards else 1.0
    values = jax.random.normal(rng, shape, jnp.float32) * scale * level
    return jnp.minimum(jnp.maximum(values, -reach), reach).astype(held_as)


def setup_inputs(seed: int = 0) -> dict:
    key_list = jax.random.split(jax.random.key(seed), 14)
    image_hidden = draw_image_hidden(jax.random.fold_in(key_list[13], 71), 0)
    text_hidden = normal_values(key_list[1], (2, REQ, TXT, D), 1.0, 6.0, ((0, 2), (1, 8), (2, 16)))
    modulation = draw_modulation(jax.random.fold_in(key_list[13], 71), 0)
    attn_weight = draw_attn_weight(jax.random.fold_in(key_list[13], 71), 0)
    proj_weight = normal_values(key_list[4], (HEADS * HEAD, D), (HEADS * HEAD) ** -0.5, 0.1875)
    mlp_in_weight = normal_values(key_list[5], (D, FF), D ** -0.5, 0.15625, ((1, 16),))
    mlp_out_weight = normal_values(key_list[6], (FF, D), FF ** -0.5, 0.078125, ((0, 16),))
    final_weight = normal_values(key_list[7], (PATCH, D), D ** -0.5, 0.15625)
    latents = normal_values(key_list[8], (REQ, PATCH, IMG), 1.0, 6.0, ((0, 8), (1, 2), (2, 16)), jnp.float32)
    guidance = jnp.clip(3.0 + 4.0 * jax.random.uniform(key_list[9], (REQ,), jnp.float32) ** levels(key_list[9], (REQ,), ((0, 8),), -0.2, 0.2), 3.0, 7.0)
    text_lengths = jax.vmap(lambda own: ragged_sizes(own, REQ, (TXT_MAX // 2) * (REQ + 1), TXT_MAX, 0))(jax.random.split(key_list[10], 2)).reshape((2, REQ)).astype(jnp.int32)
    step_index = plant(jax.random.randint(key_list[11], (REQ,), 0, STEPS), jax.random.fold_in(key_list[11], 1), 0, STEPS - 1).astype(jnp.int32)
    step_count = plant(jax.random.randint(key_list[12], (REQ,), 1, 4), jax.random.fold_in(key_list[12], 1), 1, 3).astype(jnp.int32)
    return dict(image_hidden=image_hidden, text_hidden=text_hidden, modulation=modulation, attn_weight=attn_weight, proj_weight=proj_weight, mlp_in_weight=mlp_in_weight, mlp_out_weight=mlp_out_weight, final_weight=final_weight, latents=latents, guidance=guidance, text_lengths=text_lengths, step_index=step_index, step_count=step_count)


EPS_NORM = 1e-06

def modulate(rows_in, scale_row, shift_row):
    values = rows_in.astype(jnp.float32)
    center = lax.optimization_barrier(jnp.mean(values, axis=-1, keepdims=True))
    spread = lax.optimization_barrier(jnp.mean(jnp.square(values - center), axis=-1, keepdims=True))
    return ((values - center) * lax.rsqrt(spread + EPS_NORM) * (1.0 + scale_row) + shift_row).astype(jnp.bfloat16)

def sigma_of(index):
    remain = 1.0 - index.astype(jnp.float32) / STEPS
    return 3.0 * remain / (1.0 + 2.0 * remain)

def mlp_part(hidden, mod_rows, mlp_in_weight, mlp_out_weight):
    mlp_norm = modulate(hidden, mod_rows[8], mod_rows[7])
    inner = jax.nn.gelu(jnp.dot(mlp_norm, mlp_in_weight, preferred_element_type=jnp.float32), approximate=True).astype(jnp.bfloat16)
    units = FF // N_SEQ
    inner_groups = jnp.transpose(inner.reshape(IMG, N_SEQ, units), (1, 0, 2))
    weight_groups = mlp_out_weight.reshape(N_SEQ, units, D)

    def add_group(carry, items):
        inner_group, weight_group = items
        partial_sum = jnp.dot(inner_group, weight_group, preferred_element_type=jnp.float32).astype(jnp.bfloat16)
        return (carry + partial_sum.astype(jnp.float32), None)
    mlp_out, unused = lax.scan(add_group, jnp.zeros((IMG, D), jnp.float32), (inner_groups, weight_groups))
    return hidden + mod_rows[9] * mlp_out

def branch_velocity(image_rows, text_rows, mod_rows, length, attn_weight, proj_weight, mlp_in_weight, mlp_out_weight, final_weight):
    image_norm = modulate(image_rows, mod_rows[1], mod_rows[0])
    text_norm = modulate(text_rows, mod_rows[4], mod_rows[3])
    split_cols = attn_weight.reshape(D, HEADS, 5, HEAD)
    image_cols = split_cols[:, :, 0:3, :].reshape(D, HEADS * 3 * HEAD)
    text_cols = split_cols[:, :, 3:5, :].reshape(D, HEADS * 2 * HEAD)
    image_qkv = jnp.dot(image_norm, image_cols, preferred_element_type=jnp.float32).astype(jnp.bfloat16)
    image_qkv = image_qkv.reshape(IMG, HEADS, 3, HEAD)
    text_kv = jnp.dot(text_norm, text_cols, preferred_element_type=jnp.float32).astype(jnp.bfloat16)
    text_kv = text_kv.reshape(TXT, HEADS, 2, HEAD)
    keys_all = jnp.concatenate([image_qkv[:, :, 1], text_kv[:, :, 0]], axis=0)
    values_all = jnp.concatenate([image_qkv[:, :, 2], text_kv[:, :, 1]], axis=0)
    slots = jnp.arange(TXT, dtype=jnp.int32)
    valid = jnp.concatenate([jnp.ones((IMG,), dtype=bool), slots < length])
    queries = jnp.transpose(image_qkv[:, :, 0], (1, 0, 2))
    keys_all = jnp.transpose(keys_all, (1, 0, 2))
    values_all = jnp.transpose(values_all, (1, 0, 2))

    def one_head(items):
        query_head, key_head, value_head = items
        scores = jnp.dot(query_head, key_head.T, preferred_element_type=jnp.float32) * HEAD ** (-0.5)
        scores = jnp.where(valid[None, :], scores, -1e+30)
        row_max = lax.optimization_barrier(jnp.max(scores, axis=1, keepdims=True))
        weights = jnp.exp(scores - row_max)
        total = lax.optimization_barrier(jnp.sum(weights, axis=1, keepdims=True))
        probs = weights.astype(jnp.bfloat16)
        return (jnp.dot(probs, value_head, preferred_element_type=jnp.float32) / total).astype(jnp.bfloat16)
    attended = lax.map(one_head, (queries, keys_all, values_all))
    attended = jnp.transpose(attended, (1, 0, 2)).reshape(IMG, HEADS * HEAD)
    hidden = image_rows.astype(jnp.float32) + mod_rows[2] * jnp.dot(attended, proj_weight, preferred_element_type=jnp.float32)
    block_out = mlp_part(hidden, mod_rows, mlp_in_weight, mlp_out_weight)
    final_norm = modulate(block_out, mod_rows[6], mod_rows[5])
    return jnp.dot(final_weight, final_norm.T, preferred_element_type=jnp.float32)

def reference(image_hidden, text_hidden, modulation, attn_weight, proj_weight, mlp_in_weight, mlp_out_weight, final_weight, latents, guidance, text_lengths, step_index, step_count):

    def per_request(items):
        image_pair, text_pair, mod_pair, length_pair, guide_one, latent_one, index_one, count_one = items
        cond_vel = branch_velocity(image_pair[0], text_pair[0], mod_pair[0], length_pair[0], attn_weight, proj_weight, mlp_in_weight, mlp_out_weight, final_weight)
        uncond_vel = branch_velocity(image_pair[1], text_pair[1], mod_pair[1], length_pair[1], attn_weight, proj_weight, mlp_in_weight, mlp_out_weight, final_weight)
        guided = uncond_vel + guide_one * (cond_vel - uncond_vel)
        entries = PATCH * IMG
        rms_cond = jnp.sqrt(jnp.sum(cond_vel * cond_vel) / entries + EPS_NORM)
        rms_guided = jnp.sqrt(jnp.sum(guided * guided) / entries + EPS_NORM)
        result_vel = 0.7 * (guided * (rms_cond / rms_guided)) + 0.3 * guided
        next_index = jnp.minimum(index_one + count_one, STEPS)
        step_size = sigma_of(next_index) - sigma_of(index_one)
        return (result_vel, latent_one + step_size * result_vel)
    velocity, new_latents = lax.map(per_request, (jnp.swapaxes(image_hidden, 0, 1), jnp.swapaxes(text_hidden, 0, 1), jnp.swapaxes(modulation, 0, 1), jnp.swapaxes(text_lengths, 0, 1), guidance, latents, step_index, step_count))
    return (velocity, new_latents)
```

```python
import jax
import jax.numpy as jnp
from jax import lax
from jax.sharding import Mesh, PartitionSpec as P

HEADS = 16
HEAD = 64
STEPS = 28
EPS_NORM = 1e-06
F32 = jnp.float32
BF16 = jnp.bfloat16


def xor_perm(size, mask):
    return [(i, i ^ mask) for i in range(size)]


def rot_perm(size, step):
    return [(i, (i + step) % size) for i in range(size)]


def modulate(rows_in, scale_row, shift_row):
    values = rows_in.astype(F32)
    center = jnp.mean(values, axis=-1, keepdims=True)
    spread = jnp.mean(jnp.square(values - center), axis=-1, keepdims=True)
    return (
        (values - center) * lax.rsqrt(spread + EPS_NORM) * (1.0 + scale_row) + shift_row
    ).astype(BF16)


def sigma_of(index):
    remain = 1.0 - index.astype(F32) / STEPS
    return 3.0 * remain / (1.0 + 2.0 * remain)


def dot_t(left, right):
    return lax.dot_general(left, right, (((1,), (1,)), ((), ())), preferred_element_type=F32)


def spread_pieces(pieces):
    parts = [pieces] + [lax.ppermute(pieces, "x", rot_perm(4, k)) for k in (1, 2, 3)]
    half = jnp.stack(parts)
    other = lax.ppermute(half, "core", xor_perm(2, 1))
    return half, other


def local(
    image_hidden,
    text_hidden,
    modulation,
    attn_weight,
    proj_weight,
    mlp_in_weight,
    mlp_out_weight,
    final_weight,
    latents,
    guidance,
    text_lengths,
    step_index,
    step_count,
):
    image_rows = image_hidden[0, 0]
    text_rows = text_hidden[0, 0]
    mod = modulation[0, 0]
    rows = image_rows.shape[0]
    width = image_rows.shape[1]
    text_own = text_rows.shape[0]
    x, core = lax.axis_index("x"), lax.axis_index("core")
    a, b = lax.axis_index("a"), lax.axis_index("b")
    replica = x * 2 + core

    attn_t = attn_weight.T
    image_t = attn_t[: 3 * HEAD]
    piece_rows = 3 * HEAD // 8
    own_piece = lax.dynamic_slice_in_dim(image_t, replica * piece_rows, piece_rows, 0)
    packed = jnp.concatenate([own_piece, text_rows], axis=0)
    fetched = [lax.ppermute(packed, "b", xor_perm(4, m)) for m in (1, 2, 3)]
    blocks = [image_rows] + [lax.ppermute(image_rows, "a", xor_perm(4, k)) for k in (1, 2, 3)]

    half, other = spread_pieces(jnp.stack([f[:piece_rows] for f in fetched]))
    both = jnp.stack([jnp.where(core == 0, half, other), jnp.where(core == 0, other, half)], axis=1)
    ordered = jnp.zeros_like(both)
    for k in range(4):
        ordered = lax.dynamic_update_slice_in_dim(ordered, both[k][None], (x - k) % 4, 0)
    foreign = jnp.transpose(ordered, (2, 0, 1, 3, 4)).reshape(9 * HEAD, width)
    weights_t = jnp.concatenate([image_t, foreign], axis=0)

    units = mlp_out_weight.shape[0]
    unit_piece = units // 8
    in_t = mlp_in_weight.T
    mlp_packed = jnp.concatenate(
        [
            lax.dynamic_slice_in_dim(in_t, replica * unit_piece, unit_piece, 0),
            lax.dynamic_slice_in_dim(mlp_out_weight, replica * unit_piece, unit_piece, 0),
        ],
        axis=0,
    )
    mlp_fetched = [lax.ppermute(mlp_packed, "b", xor_perm(4, m)) for m in (1, 2, 3)]
    mlp_half, mlp_other = spread_pieces(
        jnp.stack([f[:unit_piece] for f in mlp_fetched] + [f[unit_piece:] for f in mlp_fetched])
    )

    text_four = jnp.concatenate([text_rows] + [f[piece_rows:] for f in fetched], axis=0)
    text_all = jnp.concatenate(
        [text_four] + [lax.ppermute(text_four, "a", xor_perm(4, k)) for k in (1, 2, 3)], axis=0
    )
    ks = jnp.arange(4)[:, None, None]
    ms = jnp.arange(4)[None, :, None]
    slots = ((b ^ ms) * 4 + (a ^ ks)) * text_own + jnp.arange(text_own)[None, None, :]
    text_valid = (slots < text_lengths[0, 0]).reshape(-1)
    text_norm = modulate(text_all, mod[4], mod[3])
    text_kv = dot_t(attn_t[3 * HEAD :], text_norm).astype(BF16)

    hidden_in = jnp.concatenate(blocks, axis=0)
    image_norm = modulate(hidden_in, mod[1], mod[0])
    qkv = dot_t(weights_t, image_norm).astype(BF16)
    per_head = 3 * HEAD
    gathered = [qkv[:per_head]] + [
        lax.ppermute(qkv[m * per_head : (m + 1) * per_head], "b", xor_perm(4, m)) for m in (1, 2, 3)
    ]
    queries = jnp.concatenate([g[:HEAD] for g in gathered], axis=1)
    keys = jnp.concatenate([g[HEAD : 2 * HEAD] for g in gathered] + [text_kv[:HEAD]], axis=1)
    values = jnp.concatenate([g[2 * HEAD :] for g in gathered] + [text_kv[HEAD:]], axis=1)
    image_total = queries.shape[1]
    valid = jnp.concatenate([jnp.ones((image_total,), dtype=bool), text_valid])
    four_rows = 4 * rows

    def attend(query_block):
        scores = (
            lax.dot_general(query_block, keys, (((0,), (0,)), ((), ())), preferred_element_type=F32)
            * HEAD**-0.5
        )
        scores = jnp.where(valid[None, :], scores, -1e30)
        row_max = jnp.max(scores, axis=1, keepdims=True)
        weights = jnp.exp(scores - row_max)
        total = jnp.sum(weights, axis=1)
        mixed = dot_t(values, weights.astype(BF16)) / total[None, :]
        return mixed.astype(BF16)

    attended = [attend(queries[:, m * four_rows : (m + 1) * four_rows]) for m in range(4)]
    returned = jnp.concatenate(
        [attended[0]] + [lax.ppermute(attended[m], "b", xor_perm(4, m)) for m in (1, 2, 3)], axis=0
    )
    from_a = [returned] + [lax.ppermute(returned, "a", xor_perm(4, j)) for j in (1, 2, 3)]
    reordered = [
        jnp.concatenate([part[:, (j ^ k) * rows : ((j ^ k) + 1) * rows] for k in range(4)], axis=1)
        for j, part in enumerate(from_a)
    ]
    attended_all = jnp.concatenate(reordered, axis=0)
    proj_blocks = proj_weight.reshape(4, 4, HEAD, width)
    proj_rows = jnp.concatenate(
        [
            lax.dynamic_slice(proj_blocks, (b ^ m, a ^ j, 0, 0), (1, 1, HEAD, width)).reshape(HEAD, width)
            for j in range(4)
            for m in range(4)
        ],
        axis=0,
    )

    third = 3 * unit_piece
    foreign_in = jnp.concatenate([mlp_half[:, :3], mlp_other[:, :3]]).reshape(8 * third, width)
    foreign_out = jnp.concatenate([mlp_half[:, 3:], mlp_other[:, 3:]]).reshape(8 * third, width)
    all_in_t = jnp.concatenate([in_t, foreign_in], axis=0)
    all_out = jnp.concatenate([mlp_out_weight, foreign_out], axis=0)

    hidden = hidden_in.astype(F32) + mod[2] * lax.dot_general(
        attended_all, proj_rows, (((0,), (0,)), ((), ())), preferred_element_type=F32
    )
    mlp_norm = modulate(hidden, mod[8], mod[7])
    inner = jax.nn.gelu(dot_t(mlp_norm, all_in_t), approximate=True).astype(BF16)
    partial = [
        jnp.dot(inner[k * rows : (k + 1) * rows], all_out, preferred_element_type=F32).astype(BF16)
        for k in range(4)
    ]
    mlp_out = partial[0].astype(F32)
    for k in (1, 2, 3):
        mlp_out = mlp_out + lax.ppermute(partial[k], "a", xor_perm(4, k)).astype(F32)
    block_out = hidden[:rows] + mod[9] * mlp_out
    final_norm = modulate(block_out, mod[6], mod[5])
    own_vel = dot_t(final_weight, final_norm)
    partner_vel = lax.ppermute(own_vel.astype(BF16), "cfg", xor_perm(2, 1)).astype(F32)
    leading = lax.axis_index("cfg") == 0
    cond_vel = jnp.where(leading, own_vel, partner_vel)
    uncond_vel = jnp.where(leading, partner_vel, own_vel)
    guided = uncond_vel + guidance[0] * (cond_vel - uncond_vel)
    sums = jnp.stack([jnp.sum(cond_vel * cond_vel), jnp.sum(guided * guided)])
    sums = lax.all_to_all(
        jnp.broadcast_to(sums[None, :, None], (16, 2, 128)), ("b", "a"), 0, 0, tiled=True
    )
    totals = jnp.sum(sums[:, :, 0], axis=0)
    entries = own_vel.shape[0] * image_total
    rms_cond = jnp.sqrt(totals[0] / entries + EPS_NORM)
    rms_guided = jnp.sqrt(totals[1] / entries + EPS_NORM)
    result_vel = 0.7 * (guided * (rms_cond / rms_guided)) + 0.3 * guided
    channel_half = latents.shape[1]
    own_channels = lax.dynamic_slice_in_dim(
        result_vel, lax.axis_index("cfg") * channel_half, channel_half, 0
    )
    next_index = jnp.minimum(step_index[0] + step_count[0], STEPS)
    step_size = sigma_of(next_index) - sigma_of(step_index[0])
    moved = latents[0] + step_size * own_channels
    return (own_channels[None], moved[None])


def solution(mesh):
    split = Mesh(mesh.devices.reshape(2, 4, 2, 4, 4), ("cfg", "x", "core", "b", "a"))
    req, seq = ("x", "core"), ("b", "a")
    in_specs = (
        P("cfg", req, seq, None),
        P("cfg", req, seq, None),
        P("cfg", req, None, None),
        P(None, seq),
        P(),
        P(None, seq),
        P(seq, None),
        P(),
        P(req, "cfg", seq),
        P(req),
        P("cfg", req),
        P(req),
        P(req),
    )
    out_specs = (P(req, "cfg", seq), P(req, "cfg", seq))
    return jax.shard_map(local, mesh=split, in_specs=in_specs, out_specs=out_specs, check_vma=False)
```

```python
import jax
import jax.numpy as jnp
from jax import lax
from jax.experimental import pallas as pl
from jax.experimental.pallas import tpu as pltpu
from jax.sharding import Mesh, PartitionSpec as P

HEADS = 16
HEAD = 64
STEPS = 28
EPS_NORM = 1e-06
F32 = jnp.float32
BF16 = jnp.bfloat16
Z = ("zb", "z0")
A = ("z0", "y")
SEQ = ("zb", "z0", "y")
UNIT_PIECE = 48


def xor_perm(size, mask):
    return [(i, i ^ mask) for i in range(size)]


def rot_perm(size, step):
    return [(i, (i + step) % size) for i in range(size)]


def modulate(rows_in, scale_row, shift_row):
    values = rows_in.astype(F32)
    center = jnp.mean(values, axis=-1, keepdims=True)
    spread = jnp.mean(jnp.square(values - center), axis=-1, keepdims=True)
    return (
        (values - center) * lax.rsqrt(spread + EPS_NORM) * (1.0 + scale_row) + shift_row
    ).astype(BF16)


def sigma_of(index):
    remain = 1.0 - index.astype(F32) / STEPS
    return 3.0 * remain / (1.0 + 2.0 * remain)


def dot_t(left, right):
    return lax.dot_general(left, right, (((1,), (1,)), ((), ())), preferred_element_type=F32)


def norm_rows(values, scale_row, shift_row):
    center = jnp.mean(values, axis=-1, keepdims=True)
    spread = jnp.mean(jnp.square(values - center), axis=-1, keepdims=True)
    return (
        (values - center) * lax.rsqrt(spread + EPS_NORM) * (1.0 + scale_row) + shift_row
    ).astype(BF16)


def gelu(values):
    return 0.5 * values * (1.0 + jnp.tanh(0.7978845608028654 * (values + 0.044715 * values**3)))


def mlp_kernel(
    place_ref,
    attended_ref,
    hidden_in_ref,
    mod_ref,
    own_in_ref,
    own_out_ref,
    proj_ref,
    *refs,
):
    pieces, (partial_ref, hidden_ref, proj, far_in, far_out, mixed_rows, hidden, norm, inner, sems) = (
        refs[:4],
        refs[4:],
    )
    place = place_ref[0]
    copies = []

    def start(source, target):
        copy = pltpu.make_async_copy(source, target, sems.at[len(copies)])
        copy.start()
        copies.append(copy)

    for j in range(4):
        for m in range(4):
            block = place ^ (4 * m + (j & 1) * 2 + (j >> 1))
            start(proj_ref.at[block], proj.at[pl.ds((4 * j + m) * HEAD, HEAD)])
    proj_copies = len(copies)
    base = 0
    for ref in pieces:
        count = ref.shape[0]
        start(ref.at[:, 0], far_in.at[pl.ds(base, count)])
        start(ref.at[:, 1], far_out.at[pl.ds(base, count)])
        base += count
    mixed_rows[...] = attended_ref[...].T

    for copy in copies[:proj_copies]:
        copy.wait()
    width = partial_ref.shape[1]
    rows = partial_ref.shape[0]
    tile = 384
    tiles = width // tile

    @pl.loop(0, tiles)
    def _(i):
        cols = pl.ds(pl.multiple_of(i * tile, tile), tile)
        mixed = jnp.dot(mixed_rows[...], proj[:, cols], preferred_element_type=F32)
        hidden[:, cols] = hidden_in_ref[:, cols].astype(F32) + mod_ref[2:3, cols] * mixed

    hidden_ref[...] = hidden[: rows // 4]

    @pl.loop(0, rows // 64)
    def _(i):
        part = pl.ds(pl.multiple_of(i * 64, 64), 64)
        norm[part, :] = norm_rows(hidden[part, :], mod_ref[8:9, :], mod_ref[7:8, :])

    units = own_in_ref.shape[1]
    inner[:, :units] = gelu(
        jnp.dot(norm[...], own_in_ref[...], preferred_element_type=F32)
    ).astype(BF16)
    for copy in copies[proj_copies:]:
        copy.wait()

    group = tile // far_in.shape[1]

    @pl.loop(0, far_in.shape[0] // group)
    def _(i):
        part = far_in[pl.ds(i * group, group)].reshape(tile, width)
        inner[:, pl.ds(pl.multiple_of(units + i * tile, 128), tile)] = gelu(
            dot_t(norm[...], part)
        ).astype(BF16)

    @pl.loop(0, tiles)
    def _(i):
        cols = pl.ds(pl.multiple_of(i * tile, tile), tile)
        partial_ref[:, cols] = (
            jnp.dot(inner[:, :units], own_out_ref[:, cols], preferred_element_type=F32)
            + jnp.dot(
                inner[:, units:],
                far_out[:, :, cols].reshape(-1, tile),
                preferred_element_type=F32,
            )
        ).astype(BF16)


def project_and_mlp(place, attended, hidden_in, mod, own_in, own_out, proj_weight, pieces):
    rows, width = hidden_in.shape
    units = own_in.shape[1]
    far = 3 * units
    vmem = pl.BlockSpec(memory_space=pltpu.VMEM)
    anywhere = pl.BlockSpec(memory_space=pl.ANY)
    return pl.pallas_call(
        mlp_kernel,
        in_specs=[pl.BlockSpec(memory_space=pltpu.SMEM)] + [vmem] * 5 + [anywhere] * 5,
        out_specs=[vmem] * 2,
        out_shape=[
            jax.ShapeDtypeStruct((rows, width), BF16),
            jax.ShapeDtypeStruct((rows // 4, width), F32),
        ],
        scratch_shapes=[
            pltpu.VMEM((HEADS * HEAD, width), BF16),
            pltpu.VMEM((far // UNIT_PIECE, UNIT_PIECE, width), BF16),
            pltpu.VMEM((far // UNIT_PIECE, UNIT_PIECE, width), BF16),
            pltpu.VMEM((rows, HEADS * HEAD), BF16),
            pltpu.VMEM((rows, width), F32),
            pltpu.VMEM((rows, width), BF16),
            pltpu.VMEM((rows, units + far), BF16),
            pltpu.SemaphoreType.DMA((64,)),
        ],
        compiler_params=pltpu.CompilerParams(vmem_limit_bytes=40 * 2**20),
        cost_estimate=pl.CostEstimate(
            flops=2 * rows * width * (HEADS * HEAD + 2 * (units + far)),
            bytes_accessed=20 * 2**20,
            transcendentals=rows * (units + far),
        ),
    )(
        place[None],
        attended,
        hidden_in,
        mod,
        own_in,
        own_out,
        proj_weight.reshape(HEADS, HEAD, width),
        *pieces,
    )


def after(value, *earlier):
    return lax.optimization_barrier((value, earlier))[0]


def local(
    image_hidden,
    text_hidden,
    modulation,
    attn_weight,
    proj_weight,
    mlp_in_weight,
    mlp_out_weight,
    final_weight,
    latents,
    guidance,
    text_lengths,
    step_index,
    step_count,
):
    image_rows = image_hidden[0, 0]
    text_rows = text_hidden[0, 0]
    mod = modulation[0, 0]
    rows = image_rows.shape[0]
    width = image_rows.shape[1]
    text_own = text_rows.shape[0]
    replica = lax.axis_index("x") * 2 + lax.axis_index("core")
    z, y = lax.axis_index(Z), lax.axis_index("y")
    ahead, back = rot_perm(8, 1), rot_perm(8, -1)
    swap = xor_perm(2, 1)

    text_pad = 16
    packed = jnp.concatenate(
        [image_rows, jnp.pad(text_rows, ((0, text_pad - text_own), (0, 0)))], axis=0
    )
    up, down = [packed], [packed]
    for _ in range(3):
        up.append(lax.ppermute(up[-1], Z, ahead))
        down.append(lax.ppermute(down[-1], Z, back))
    cut = rows // 2
    far_low = lax.ppermute(up[3][:cut], Z, ahead)
    far_high = lax.ppermute(down[3][cut:], Z, back)
    far = jnp.concatenate([far_low, far_high], axis=0)
    other_weight = lax.ppermute(attn_weight, "y", swap)

    units = mlp_out_weight.shape[0]
    unit_piece = units // 8
    mlp_packed = jnp.concatenate(
        [
            lax.dynamic_slice_in_dim(mlp_in_weight, replica * unit_piece, unit_piece, 1).T,
            lax.dynamic_slice_in_dim(mlp_out_weight, replica * unit_piece, unit_piece, 0),
        ],
        axis=0,
    )
    mlp_packed = after(mlp_packed, far)
    mlp_fetched = [lax.ppermute(mlp_packed, "zb", xor_perm(4, m)) for m in (1, 2, 3)]

    per_head = 3 * HEAD
    own_t, other_t = attn_weight.T, other_weight.T
    image_t = jnp.concatenate([own_t[:per_head], other_t[:per_head]], axis=0)
    text_t = jnp.concatenate([own_t[per_head:], other_t[per_head:]], axis=0)

    def project(parts):
        norm = modulate(jnp.concatenate([part[:rows] for part in parts], axis=0), mod[1], mod[0])
        return dot_t(image_t, norm).astype(BF16)

    by_step = [project([packed])]
    by_step += [project([up[k], down[k]]) for k in (1, 2, 3)]
    by_step.append(project([far]))
    image_qkv = jnp.zeros((2 * per_head, 8 * rows), BF16)
    offsets = [0]
    for k, piece in enumerate(by_step):
        steps = [-k, k] if k in (1, 2, 3) else [k]
        for i, offset in enumerate(steps):
            if k:
                offsets.append(offset)
            image_qkv = lax.dynamic_update_slice_in_dim(
                image_qkv, piece[:, i * rows : (i + 1) * rows], (((z + offset) % 8) ^ z) * rows, 1
            )
    text_parts = [packed] + [part for k in (1, 2, 3) for part in (up[k], down[k])] + [far]
    text_norm = modulate(jnp.concatenate([p[rows:] for p in text_parts], axis=0), mod[4], mod[3])
    text_kv = dot_t(text_t, text_norm).astype(BF16)
    send = jnp.concatenate(
        [image_qkv[per_head:], jnp.pad(text_kv[2 * HEAD :], ((HEAD, 0), (0, 0)))], axis=1
    )
    got = lax.ppermute(send, "y", swap)

    z_of = (z + jnp.array(offsets, jnp.int32)) % 8
    slots = (z_of[None, :] * 2 + (y ^ jnp.arange(2))[:, None])[:, :, None] * text_own
    in_pad = jnp.arange(text_pad)
    text_valid = (slots + in_pad < text_lengths[0, 0]) & (in_pad < text_own)
    text_valid = text_valid.reshape(2, 8 * text_pad)
    image_half = 8 * rows
    image_total = 2 * image_half
    valid = jnp.concatenate(
        [jnp.ones((image_half,), bool), text_valid[0], jnp.ones((image_half,), bool), text_valid[1]]
    )

    keys = jnp.concatenate(
        [image_qkv[HEAD : 2 * HEAD], text_kv[:HEAD], got[HEAD : 2 * HEAD]], axis=1
    )
    values = jnp.concatenate(
        [image_qkv[2 * HEAD : per_head], text_kv[HEAD : 2 * HEAD], got[2 * HEAD :]], axis=1
    )
    near = after(jnp.where(z % 2 == 0, down[1][:rows], up[1][:rows]), got)
    pair_rows = jnp.concatenate([image_rows, near], axis=0)
    hidden_in = jnp.concatenate([pair_rows, lax.ppermute(pair_rows, "y", swap)], axis=0)

    def attend(query_block):
        scores = (
            lax.dot_general(query_block, keys, (((0,), (0,)), ((), ())), preferred_element_type=F32)
            * HEAD**-0.5
        )
        scores = jnp.where(valid[None, :], scores, -1e30)
        row_max = jnp.max(scores, axis=1, keepdims=True)
        weights = jnp.exp(scores - row_max)
        total = jnp.sum(weights, axis=1)
        mixed = dot_t(values, weights.astype(BF16)) / total[None, :]
        return mixed.astype(BF16)

    pair = 2 * rows
    attended = [
        attend(
            jnp.concatenate(
                [image_qkv[:HEAD, m * pair : (m + 1) * pair], got[:HEAD, m * pair : (m + 1) * pair]],
                axis=1,
            )
        )
        for m in range(4)
    ]
    returned = jnp.concatenate(
        [attended[0]] + [lax.ppermute(attended[m], "zb", xor_perm(4, m)) for m in (1, 2, 3)], axis=0
    )
    def over_x(pieces, first, second):
        pieces = after(pieces, first)
        pieces = jnp.concatenate([p.reshape(1, 2, unit_piece, width) for p in pieces], axis=0)
        left = lax.ppermute(pieces, "x", rot_perm(4, 1))
        right = lax.ppermute(pieces, "x", rot_perm(4, -1))
        left, right = after((left, right), second)
        far_in = lax.ppermute(left[:, 0], "x", rot_perm(4, 1))
        far_out = lax.ppermute(right[:, 1], "x", rot_perm(4, -1))
        far = jnp.stack([far_in, far_out], axis=1)
        half = jnp.concatenate([pieces, left, right, far], axis=0)
        return half, lax.ppermute(half, "core", swap)

    near_half, near_other = over_x(mlp_fetched[::2], attended[0], attended[3])
    far_half, far_other = over_x(mlp_fetched[1:2], attended[2], returned)

    groups = [xor_perm(4, (k & 1) * 2 + (k >> 1)) for k in range(4)]
    from_a = [returned] + [lax.ppermute(returned, A, groups[j]) for j in (1, 2, 3)]
    reordered = [
        jnp.concatenate([part[:, (j ^ k) * rows : ((j ^ k) + 1) * rows] for k in range(4)], axis=1)
        for j, part in enumerate(from_a)
    ]
    partial, own_hidden = project_and_mlp(
        z * 2 + y,
        jnp.concatenate(reordered, axis=0),
        hidden_in,
        mod,
        mlp_in_weight,
        mlp_out_weight,
        proj_weight,
        [near_half, far_half, near_other, far_other],
    )
    mlp_out = partial[:rows].astype(F32)
    for k in (1, 2, 3):
        mlp_out = mlp_out + lax.ppermute(partial[k * rows : (k + 1) * rows], A, groups[k]).astype(F32)
    block_out = own_hidden + mod[9] * mlp_out
    final_norm = modulate(block_out, mod[6], mod[5])
    own_vel = dot_t(final_weight, final_norm)
    partner_vel = lax.ppermute(own_vel.astype(BF16), "cfg", xor_perm(2, 1)).astype(F32)
    leading = lax.axis_index("cfg") == 0
    cond_vel = jnp.where(leading, own_vel, partner_vel)
    uncond_vel = jnp.where(leading, partner_vel, own_vel)
    guided = uncond_vel + guidance[0] * (cond_vel - uncond_vel)
    first_row = lax.broadcasted_iota(jnp.int32, (16, 2, 128), 1) == 0
    sums = jnp.where(first_row, jnp.sum(cond_vel * cond_vel), jnp.sum(guided * guided))
    sums = lax.all_to_all(sums, SEQ, 0, 0, tiled=True)
    totals = jnp.sum(sums[:, :, 0], axis=0)
    entries = own_vel.shape[0] * image_total
    rms_cond = jnp.sqrt(totals[0] / entries + EPS_NORM)
    rms_guided = jnp.sqrt(totals[1] / entries + EPS_NORM)
    result_vel = 0.7 * (guided * (rms_cond / rms_guided)) + 0.3 * guided
    channel_half = latents.shape[1]
    own_channels = lax.dynamic_slice_in_dim(
        result_vel, lax.axis_index("cfg") * channel_half, channel_half, 0
    )
    next_index = jnp.minimum(step_index[0] + step_count[0], STEPS)
    step_size = sigma_of(next_index) - sigma_of(step_index[0])
    moved = latents[0] + step_size * own_channels
    return (own_channels[None], moved[None])


def solution(mesh):
    split = Mesh(mesh.devices.reshape(2, 4, 2, 4, 2, 2), ("cfg", "x", "core", "zb", "z0", "y"))
    req, seq = ("x", "core"), SEQ
    in_specs = (
        P("cfg", req, seq, None),
        P("cfg", req, seq, None),
        P("cfg", req, None, None),
        P(None, seq),
        P(),
        P(None, seq),
        P(seq, None),
        P(),
        P(req, "cfg", seq),
        P(req),
        P("cfg", req),
        P(req),
        P(req),
    )
    out_specs = (P(req, "cfg", seq), P(req, "cfg", seq))
    return jax.shard_map(local, mesh=split, in_specs=in_specs, out_specs=out_specs, check_vma=False)
```

```python
import jax
import jax.numpy as jnp
from jax import lax
from jax.experimental import pallas as pl
from jax.experimental.pallas import tpu as pltpu
from jax.sharding import Mesh, PartitionSpec as P

HEADS = 16
HEAD = 64
STEPS = 28
EPS_NORM = 1e-06
F32 = jnp.float32
BF16 = jnp.bfloat16
Z = ("zb", "z0")
A = ("z0", "y")
SEQ = ("zb", "z0", "y")
UNIT_PIECE = 48


def xor_perm(size, mask):
    return [(i, i ^ mask) for i in range(size)]


def rot_perm(size, step):
    return [(i, (i + step) % size) for i in range(size)]


def modulate(rows_in, scale_row, shift_row):
    values = rows_in.astype(F32)
    center = jnp.mean(values, axis=-1, keepdims=True)
    spread = jnp.mean(jnp.square(values - center), axis=-1, keepdims=True)
    return (
        (values - center) * lax.rsqrt(spread + EPS_NORM) * (1.0 + scale_row) + shift_row
    ).astype(BF16)


def sigma_of(index):
    remain = 1.0 - index.astype(F32) / STEPS
    return 3.0 * remain / (1.0 + 2.0 * remain)


def dot_t(left, right):
    return lax.dot_general(left, right, (((1,), (1,)), ((), ())), preferred_element_type=F32)


def norm_rows(values, scale_row, shift_row):
    center = jnp.mean(values, axis=-1, keepdims=True)
    spread = jnp.mean(jnp.square(values - center), axis=-1, keepdims=True)
    return (
        (values - center) * lax.rsqrt(spread + EPS_NORM) * (1.0 + scale_row) + shift_row
    ).astype(BF16)


def gelu(values):
    return 0.5 * values * (1.0 + jnp.tanh(0.7978845608028654 * (values + 0.044715 * values**3)))


def project_kernel(
    place_ref,
    attended_ref,
    hidden_in_ref,
    mod_ref,
    own_in_ref,
    proj_ref,
    norm_ref,
    inner_ref,
    hidden_ref,
    proj,
    mixed_rows,
    hidden,
    sems,
):
    place = place_ref[0]
    copies = []
    for j in range(4):
        for m in range(4):
            block = place ^ (4 * m + (j & 1) * 2 + (j >> 1))
            target = proj.at[pl.ds((4 * j + m) * HEAD, HEAD)]
            copies.append(pltpu.make_async_copy(proj_ref.at[block], target, sems.at[4 * j + m]))
            copies[-1].start()
    mixed_rows[...] = attended_ref[...].T
    for copy in copies:
        copy.wait()
    rows, width = norm_ref.shape
    tile = 384

    @pl.loop(0, width // tile)
    def _(i):
        cols = pl.ds(pl.multiple_of(i * tile, tile), tile)
        mixed = jnp.dot(mixed_rows[...], proj[:, cols], preferred_element_type=F32)
        hidden[:, cols] = hidden_in_ref[:, cols].astype(F32) + mod_ref[2:3, cols] * mixed

    hidden_ref[...] = hidden[: rows // 4]

    @pl.loop(0, rows // 64)
    def _(i):
        part = pl.ds(pl.multiple_of(i * 64, 64), 64)
        norm_ref[part, :] = norm_rows(hidden[part, :], mod_ref[8:9, :], mod_ref[7:8, :])

    inner_ref[...] = gelu(
        jnp.dot(norm_ref[...], own_in_ref[...], preferred_element_type=F32)
    ).astype(BF16)


def mlp_kernel(norm_ref, inner_own_ref, own_out_ref, *refs):
    pieces, (partial_ref, far_in, far_out, inner, sems) = refs[:4], refs[4:]
    copies = []
    base = 0
    for ref in pieces:
        count = ref.shape[0]
        for side, target in enumerate((far_in, far_out)):
            copies.append(
                pltpu.make_async_copy(
                    ref.at[:, side], target.at[pl.ds(base, count)], sems.at[len(copies)]
                )
            )
            copies[-1].start()
        base += count
    for copy in copies:
        copy.wait()
    width = partial_ref.shape[1]
    tile = 384
    group = tile // far_in.shape[1]

    @pl.loop(0, far_in.shape[0] // group)
    def _(i):
        part = far_in[pl.ds(i * group, group)].reshape(tile, width)
        inner[:, pl.ds(pl.multiple_of(i * tile, tile), tile)] = gelu(
            dot_t(norm_ref[...], part)
        ).astype(BF16)

    @pl.loop(0, width // tile)
    def _(i):
        cols = pl.ds(pl.multiple_of(i * tile, tile), tile)
        partial_ref[:, cols] = (
            jnp.dot(inner_own_ref[...], own_out_ref[:, cols], preferred_element_type=F32)
            + jnp.dot(
                inner[...], far_out[:, :, cols].reshape(-1, tile), preferred_element_type=F32
            )
        ).astype(BF16)


VMEM = pl.BlockSpec(memory_space=pltpu.VMEM)
ANYWHERE = pl.BlockSpec(memory_space=pl.ANY)


def project_rows(place, attended, hidden_in, mod, own_in, proj_weight):
    rows, width = hidden_in.shape
    units = own_in.shape[1]
    return pl.pallas_call(
        project_kernel,
        in_specs=[pl.BlockSpec(memory_space=pltpu.SMEM)] + [VMEM] * 4 + [ANYWHERE],
        out_specs=[VMEM] * 3,
        out_shape=[
            jax.ShapeDtypeStruct((rows, width), BF16),
            jax.ShapeDtypeStruct((rows, units), BF16),
            jax.ShapeDtypeStruct((rows // 4, width), F32),
        ],
        scratch_shapes=[
            pltpu.VMEM((HEADS * HEAD, width), BF16),
            pltpu.VMEM((rows, HEADS * HEAD), BF16),
            pltpu.VMEM((rows, width), F32),
            pltpu.SemaphoreType.DMA((HEADS,)),
        ],
        compiler_params=pltpu.CompilerParams(vmem_limit_bytes=32 * 2**20),
        cost_estimate=pl.CostEstimate(
            flops=2 * rows * width * (HEADS * HEAD + units),
            bytes_accessed=10 * 2**20,
            transcendentals=rows * units,
        ),
    )(place[None], attended, hidden_in, mod, own_in, proj_weight.reshape(HEADS, HEAD, width))


def mlp_rows(norm, inner_own, own_out, pieces):
    rows, width = norm.shape
    far = 3 * own_out.shape[0]
    return pl.pallas_call(
        mlp_kernel,
        in_specs=[VMEM] * 3 + [ANYWHERE] * 4,
        out_specs=VMEM,
        out_shape=jax.ShapeDtypeStruct((rows, width), BF16),
        scratch_shapes=[
            pltpu.VMEM((far // UNIT_PIECE, UNIT_PIECE, width), BF16),
            pltpu.VMEM((far // UNIT_PIECE, UNIT_PIECE, width), BF16),
            pltpu.VMEM((rows, far), BF16),
            pltpu.SemaphoreType.DMA((8,)),
        ],
        compiler_params=pltpu.CompilerParams(vmem_limit_bytes=32 * 2**20),
        cost_estimate=pl.CostEstimate(
            flops=4 * rows * width * far,
            bytes_accessed=12 * 2**20,
            transcendentals=rows * far,
        ),
    )(norm, inner_own, own_out, *pieces)


def after(value, *earlier):
    return lax.optimization_barrier((value, earlier))[0]


def local(
    image_hidden,
    text_hidden,
    modulation,
    attn_weight,
    proj_weight,
    mlp_in_weight,
    mlp_out_weight,
    final_weight,
    latents,
    guidance,
    text_lengths,
    step_index,
    step_count,
):
    image_rows = image_hidden[0, 0]
    text_rows = text_hidden[0, 0]
    mod = modulation[0, 0]
    rows = image_rows.shape[0]
    width = image_rows.shape[1]
    text_own = text_rows.shape[0]
    replica = lax.axis_index("x") * 2 + lax.axis_index("core")
    z, y = lax.axis_index(Z), lax.axis_index("y")
    ahead, back = rot_perm(8, 1), rot_perm(8, -1)
    swap = xor_perm(2, 1)

    text_pad = 16
    packed = jnp.concatenate(
        [image_rows, jnp.pad(text_rows, ((0, text_pad - text_own), (0, 0)))], axis=0
    )
    units = mlp_out_weight.shape[0]
    unit_piece = units // 8
    mlp_packed = jnp.concatenate(
        [
            lax.dynamic_slice_in_dim(mlp_in_weight, replica * unit_piece, unit_piece, 1).T,
            lax.dynamic_slice_in_dim(mlp_out_weight, replica * unit_piece, unit_piece, 0),
        ],
        axis=0,
    )
    up, down = [packed], [packed]
    for k in range(3):
        if k == 1:
            up[1], down[1] = after((up[1], down[1]), mlp_packed)
        up.append(lax.ppermute(up[-1], Z, ahead))
        down.append(lax.ppermute(down[-1], Z, back))
    cut = rows // 2
    far_low = lax.ppermute(up[3][:cut], Z, ahead)
    far_high = lax.ppermute(down[3][cut:], Z, back)
    far = jnp.concatenate([far_low, far_high], axis=0)
    other_weight = lax.ppermute(attn_weight, "y", swap)

    per_head = 3 * HEAD
    own_t, other_t = after((attn_weight, other_weight), up[1], down[1])
    own_t, other_t = own_t.T, other_t.T
    image_t = jnp.concatenate([own_t[:per_head], other_t[:per_head]], axis=0)
    text_t = jnp.concatenate([own_t[per_head:], other_t[per_head:]], axis=0)

    def project(parts):
        norm = modulate(jnp.concatenate([part[:rows] for part in parts], axis=0), mod[1], mod[0])
        return dot_t(image_t, norm).astype(BF16)

    by_step = [project([packed, up[1], down[1]]), project([up[2], down[2]])]
    near = after(jnp.where(z % 2 == 0, down[1][:rows], up[1][:rows]), by_step[0])
    pair_rows = jnp.concatenate([image_rows, near], axis=0)
    hidden_in = jnp.concatenate([pair_rows, lax.ppermute(pair_rows, "y", swap)], axis=0)

    by_step.append(project([up[3], after(down[3], far, hidden_in), far]))
    offsets = [0, -1, 1, -2, 2, -3, 3, 4]
    text_parts = [packed] + [part for k in (1, 2, 3) for part in (up[k], down[k])] + [far]
    text_norm = modulate(jnp.concatenate([p[rows:] for p in text_parts], axis=0), mod[4], mod[3])
    text_kv = dot_t(text_t, text_norm).astype(BF16)
    text_kv = jnp.concatenate(
        [jnp.pad(part, ((HEAD, 0), (0, 0))) for part in (text_kv[: 2 * HEAD], text_kv[2 * HEAD :])]
    )
    all_qkv = jnp.concatenate([by_step[0], by_step[1], by_step[2], text_kv], axis=1)
    in_order = all_qkv
    for i, offset in enumerate(offsets[1:7]):
        piece = all_qkv[:, (i + 1) * rows : (i + 2) * rows]
        in_order = lax.dynamic_update_slice_in_dim(
            in_order, piece, (((z + offset) % 8) ^ z) * rows, 1
        )
    in_order = lax.dynamic_update_slice_in_dim(
        in_order, all_qkv[:, 7 * rows : 8 * rows], 4 * rows, 1
    )
    send = in_order[per_head:]
    got = lax.ppermute(send, "y", swap)
    mlp_packed = after(mlp_packed, send)
    mlp_fetched = [lax.ppermute(mlp_packed, "zb", xor_perm(4, m)) for m in (1, 2, 3)]


    z_of = (z + jnp.array(offsets, jnp.int32)) % 8
    slots = (z_of[None, :] * 2 + (y ^ jnp.arange(2))[:, None])[:, :, None] * text_own
    in_pad = jnp.arange(text_pad)
    text_valid = (slots + in_pad < text_lengths[0, 0]) & (in_pad < text_own)
    text_valid = text_valid.reshape(2, 8 * text_pad)
    image_total = 16 * rows
    always = jnp.ones((8 * rows,), bool)
    valid = jnp.concatenate([always, text_valid[0], always, text_valid[1]])

    mine = in_order[:per_head]
    keys = jnp.concatenate([mine[HEAD : 2 * HEAD], got[HEAD : 2 * HEAD]], axis=1)
    values = jnp.concatenate([mine[2 * HEAD :], got[2 * HEAD :]], axis=1)
    def attend(query_block):
        scores = (
            lax.dot_general(query_block, keys, (((0,), (0,)), ((), ())), preferred_element_type=F32)
            * HEAD**-0.5
        )
        scores = jnp.where(valid[None, :], scores, -1e30)
        row_max = jnp.max(scores, axis=1, keepdims=True)
        weights = jnp.exp(scores - row_max)
        total = jnp.sum(weights, axis=1)
        mixed = dot_t(values, weights.astype(BF16)) / total[None, :]
        return mixed.astype(BF16)

    pair = 2 * rows
    attended = [
        attend(
            jnp.concatenate([part[:HEAD, m * pair : (m + 1) * pair] for part in (mine, got)], axis=1)
        )
        for m in range(4)
    ]
    returned = jnp.concatenate(
        [attended[0]] + [lax.ppermute(attended[m], "zb", xor_perm(4, m)) for m in (1, 2, 3)], axis=0
    )
    groups = [xor_perm(4, (k & 1) * 2 + (k >> 1)) for k in range(4)]
    from_a = [returned] + [lax.ppermute(returned, A, groups[j]) for j in (1, 2, 3)]

    mlp_fetched = after(mlp_fetched, *attended)
    mlp_pieces = jnp.concatenate(
        [p.reshape(1, 2, unit_piece, width) for p in mlp_fetched], axis=0
    )
    left = lax.ppermute(mlp_pieces, "x", rot_perm(4, 1))
    right = lax.ppermute(mlp_pieces, "x", rot_perm(4, -1))
    left, right = after((left, right), *from_a)
    near_half = jnp.concatenate([mlp_pieces, left, right], axis=0)
    near_other = lax.ppermute(near_half, "core", swap)
    far_in = lax.ppermute(left[:, 0], "x", rot_perm(4, 1))
    far_out = lax.ppermute(right[:, 1], "x", rot_perm(4, -1))
    reordered = [
        jnp.concatenate([part[:, (j ^ k) * rows : ((j ^ k) + 1) * rows] for k in range(4)], axis=1)
        for j, part in enumerate(from_a)
    ]
    mlp_norm, inner_own, own_hidden = project_rows(
        z * 2 + y, jnp.concatenate(reordered, axis=0), hidden_in, mod, mlp_in_weight, proj_weight
    )
    far_in, far_out = after((far_in, far_out), mlp_norm)
    far_half = jnp.stack([far_in, far_out], axis=1)
    far_other = lax.ppermute(far_half, "core", swap)
    partial = mlp_rows(
        mlp_norm, inner_own, mlp_out_weight, [near_half, far_half, near_other, far_other]
    )
    mlp_out = partial[:rows].astype(F32)
    for k in (1, 2, 3):
        mlp_out = mlp_out + lax.ppermute(partial[k * rows : (k + 1) * rows], A, groups[k]).astype(F32)
    block_out = own_hidden + mod[9] * mlp_out
    final_norm = modulate(block_out, mod[6], mod[5])
    own_vel = dot_t(final_weight, final_norm)
    partner_vel = lax.ppermute(own_vel.astype(BF16), "cfg", xor_perm(2, 1)).astype(F32)
    leading = lax.axis_index("cfg") == 0
    cond_vel = jnp.where(leading, own_vel, partner_vel)
    uncond_vel = jnp.where(leading, partner_vel, own_vel)
    guided = uncond_vel + guidance[0] * (cond_vel - uncond_vel)
    first_row = lax.broadcasted_iota(jnp.int32, (16, 2, 128), 1) == 0
    sums = jnp.where(first_row, jnp.sum(cond_vel * cond_vel), jnp.sum(guided * guided))
    sums = lax.all_to_all(sums, SEQ, 0, 0, tiled=True)
    totals = jnp.sum(sums[:, :, 0], axis=0)
    entries = own_vel.shape[0] * image_total
    rms_cond = jnp.sqrt(totals[0] / entries + EPS_NORM)
    rms_guided = jnp.sqrt(totals[1] / entries + EPS_NORM)
    result_vel = 0.7 * (guided * (rms_cond / rms_guided)) + 0.3 * guided
    channel_half = latents.shape[1]
    own_channels = lax.dynamic_slice_in_dim(
        result_vel, lax.axis_index("cfg") * channel_half, channel_half, 0
    )
    next_index = jnp.minimum(step_index[0] + step_count[0], STEPS)
    step_size = sigma_of(next_index) - sigma_of(step_index[0])
    moved = latents[0] + step_size * own_channels
    return (own_channels[None], moved[None])


def solution(mesh):
    split = Mesh(mesh.devices.reshape(2, 4, 2, 4, 2, 2), ("cfg", "x", "core", "zb", "z0", "y"))
    req, seq = ("x", "core"), SEQ
    in_specs = (
        P("cfg", req, seq, None),
        P("cfg", req, seq, None),
        P("cfg", req, None, None),
        P(None, seq),
        P(),
        P(None, seq),
        P(seq, None),
        P(),
        P(req, "cfg", seq),
        P(req),
        P("cfg", req),
        P(req),
        P(req),
    )
    out_specs = (P(req, "cfg", seq), P(req, "cfg", seq))
    return jax.shard_map(local, mesh=split, in_specs=in_specs, out_specs=out_specs, check_vma=False)
```

```python
import jax
import jax.numpy as jnp
from jax import lax
from jax.experimental import pallas as pl
from jax.experimental.pallas import tpu as pltpu
from jax.sharding import Mesh, PartitionSpec as P

HEADS = 16
HEAD = 64
STEPS = 28
EPS_NORM = 1e-06
F32 = jnp.float32
BF16 = jnp.bfloat16
Z = ("zb", "z0")
A = ("z0", "y")
SEQ = ("zb", "z0", "y")
UNIT_PIECE = 48


def xor_perm(size, mask):
    return [(i, i ^ mask) for i in range(size)]


def rot_perm(size, step):
    return [(i, (i + step) % size) for i in range(size)]


def modulate(rows_in, scale_row, shift_row):
    values = rows_in.astype(F32)
    center = jnp.mean(values, axis=-1, keepdims=True)
    spread = jnp.mean(jnp.square(values - center), axis=-1, keepdims=True)
    return (
        (values - center) * lax.rsqrt(spread + EPS_NORM) * (1.0 + scale_row) + shift_row
    ).astype(BF16)


def sigma_of(index):
    remain = 1.0 - index.astype(F32) / STEPS
    return 3.0 * remain / (1.0 + 2.0 * remain)


def dot_t(left, right):
    return lax.dot_general(left, right, (((1,), (1,)), ((), ())), preferred_element_type=F32)


def norm_rows(values, scale_row, shift_row):
    center = jnp.mean(values, axis=-1, keepdims=True)
    spread = jnp.mean(jnp.square(values - center), axis=-1, keepdims=True)
    return (
        (values - center) * lax.rsqrt(spread + EPS_NORM) * (1.0 + scale_row) + shift_row
    ).astype(BF16)


def gelu(values):
    return 0.5 * values * (1.0 + jnp.tanh(0.7978845608028654 * (values + 0.044715 * values**3)))


def project_kernel(
    place_ref,
    attended_ref,
    hidden_in_ref,
    mod_ref,
    own_in_ref,
    proj_ref,
    norm_ref,
    inner_ref,
    hidden_ref,
    proj,
    mixed_rows,
    hidden,
    sems,
):
    place = place_ref[0]
    copies = []
    for j in range(4):
        for m in range(4):
            block = place ^ (4 * m + (j & 1) * 2 + (j >> 1))
            target = proj.at[pl.ds((4 * j + m) * HEAD, HEAD)]
            copies.append(pltpu.make_async_copy(proj_ref.at[block], target, sems.at[4 * j + m]))
            copies[-1].start()
    mixed_rows[...] = attended_ref[...].T
    for copy in copies:
        copy.wait()
    rows, width = norm_ref.shape
    tile = 384

    @pl.loop(0, width // tile)
    def _(i):
        cols = pl.ds(pl.multiple_of(i * tile, tile), tile)
        mixed = jnp.dot(mixed_rows[...], proj[:, cols], preferred_element_type=F32)
        hidden[:, cols] = hidden_in_ref[:, cols].astype(F32) + mod_ref[2:3, cols] * mixed

    hidden_ref[...] = hidden[: rows // 4]

    @pl.loop(0, rows // 64)
    def _(i):
        part = pl.ds(pl.multiple_of(i * 64, 64), 64)
        norm_ref[part, :] = norm_rows(hidden[part, :], mod_ref[8:9, :], mod_ref[7:8, :])

    inner_ref[...] = gelu(
        jnp.dot(norm_ref[...], own_in_ref[...], preferred_element_type=F32)
    ).astype(BF16)


def mlp_kernel(norm_ref, inner_own_ref, own_out_ref, *refs):
    pieces, (partial_ref, far_in, far_out, inner, sems) = refs[:4], refs[4:]
    copies = []
    base = 0
    for ref in pieces:
        count = ref.shape[0]
        for side, target in enumerate((far_in, far_out)):
            copies.append(
                pltpu.make_async_copy(
                    ref.at[:, side], target.at[pl.ds(base, count)], sems.at[len(copies)]
                )
            )
            copies[-1].start()
        base += count
    for copy in copies[::2]:
        copy.wait()
    width = partial_ref.shape[1]
    tile = 384
    group = tile // far_in.shape[1]

    @pl.loop(0, far_in.shape[0] // group)
    def _(i):
        part = far_in[pl.ds(i * group, group)].reshape(tile, width)
        inner[:, pl.ds(pl.multiple_of(i * tile, tile), tile)] = gelu(
            dot_t(norm_ref[...], part)
        ).astype(BF16)

    for copy in copies[1::2]:
        copy.wait()

    @pl.loop(0, width // tile)
    def _(i):
        cols = pl.ds(pl.multiple_of(i * tile, tile), tile)
        partial_ref[:, cols] = (
            jnp.dot(inner_own_ref[...], own_out_ref[:, cols], preferred_element_type=F32)
            + jnp.dot(
                inner[...], far_out[:, :, cols].reshape(-1, tile), preferred_element_type=F32
            )
        ).astype(BF16)


VMEM = pl.BlockSpec(memory_space=pltpu.VMEM)
ANYWHERE = pl.BlockSpec(memory_space=pl.ANY)


def project_rows(place, attended, hidden_in, mod, own_in, proj_weight):
    rows, width = hidden_in.shape
    units = own_in.shape[1]
    return pl.pallas_call(
        project_kernel,
        in_specs=[pl.BlockSpec(memory_space=pltpu.SMEM)] + [VMEM] * 4 + [ANYWHERE],
        out_specs=[VMEM] * 3,
        out_shape=[
            jax.ShapeDtypeStruct((rows, width), BF16),
            jax.ShapeDtypeStruct((rows, units), BF16),
            jax.ShapeDtypeStruct((rows // 4, width), F32),
        ],
        scratch_shapes=[
            pltpu.VMEM((HEADS * HEAD, width), BF16),
            pltpu.VMEM((rows, HEADS * HEAD), BF16),
            pltpu.VMEM((rows, width), F32),
            pltpu.SemaphoreType.DMA((HEADS,)),
        ],
        compiler_params=pltpu.CompilerParams(vmem_limit_bytes=32 * 2**20),
        cost_estimate=pl.CostEstimate(
            flops=2 * rows * width * (HEADS * HEAD + units),
            bytes_accessed=10 * 2**20,
            transcendentals=rows * units,
        ),
    )(place[None], attended, hidden_in, mod, own_in, proj_weight.reshape(HEADS, HEAD, width))


def mlp_rows(norm, inner_own, own_out, pieces):
    rows, width = norm.shape
    far = 3 * own_out.shape[0]
    return pl.pallas_call(
        mlp_kernel,
        in_specs=[VMEM] * 3 + [ANYWHERE] * 4,
        out_specs=VMEM,
        out_shape=jax.ShapeDtypeStruct((rows, width), BF16),
        scratch_shapes=[
            pltpu.VMEM((far // UNIT_PIECE, UNIT_PIECE, width), BF16),
            pltpu.VMEM((far // UNIT_PIECE, UNIT_PIECE, width), BF16),
            pltpu.VMEM((rows, far), BF16),
            pltpu.SemaphoreType.DMA((8,)),
        ],
        compiler_params=pltpu.CompilerParams(vmem_limit_bytes=32 * 2**20),
        cost_estimate=pl.CostEstimate(
            flops=4 * rows * width * far,
            bytes_accessed=12 * 2**20,
            transcendentals=rows * far,
        ),
    )(norm, inner_own, own_out, *pieces)


def after(value, *earlier):
    return lax.optimization_barrier((value, earlier))[0]


def local(
    image_hidden,
    text_hidden,
    modulation,
    attn_weight,
    proj_weight,
    mlp_in_weight,
    mlp_out_weight,
    final_weight,
    latents,
    guidance,
    text_lengths,
    step_index,
    step_count,
):
    image_rows = image_hidden[0, 0]
    text_rows = text_hidden[0, 0]
    mod = modulation[0, 0]
    rows = image_rows.shape[0]
    width = image_rows.shape[1]
    text_own = text_rows.shape[0]
    replica = lax.axis_index("x") * 2 + lax.axis_index("core")
    z, y = lax.axis_index(Z), lax.axis_index("y")
    ahead, back = rot_perm(8, 1), rot_perm(8, -1)
    swap = xor_perm(2, 1)

    text_pad = 16
    packed = jnp.concatenate(
        [image_rows, jnp.pad(text_rows, ((0, text_pad - text_own), (0, 0)))], axis=0
    )
    units = mlp_out_weight.shape[0]
    unit_piece = units // 8
    mlp_packed = jnp.concatenate(
        [
            lax.dynamic_slice_in_dim(mlp_in_weight, replica * unit_piece, unit_piece, 1).T,
            lax.dynamic_slice_in_dim(mlp_out_weight, replica * unit_piece, unit_piece, 0),
        ],
        axis=0,
    )
    up, down = [packed], [packed]
    for k in range(3):
        if k == 1:
            up[1], down[1] = after((up[1], down[1]), mlp_packed)
        up.append(lax.ppermute(up[-1], Z, ahead))
        down.append(lax.ppermute(down[-1], Z, back))
    cut = rows // 2
    far_low = lax.ppermute(up[3][:cut], Z, ahead)
    far_high = lax.ppermute(down[3][cut:], Z, back)
    far = jnp.concatenate([far_low, far_high], axis=0)
    other_weight = lax.ppermute(attn_weight, "y", swap)

    per_head = 3 * HEAD
    own_t, other_t = after((attn_weight, other_weight), up[1], down[1])
    own_t, other_t = own_t.T, other_t.T
    image_t = jnp.concatenate([own_t[:per_head], other_t[:per_head]], axis=0)
    text_t = jnp.concatenate([own_t[per_head:], other_t[per_head:]], axis=0)

    def project(parts):
        norm = modulate(jnp.concatenate([part[:rows] for part in parts], axis=0), mod[1], mod[0])
        return dot_t(image_t, norm).astype(BF16)

    by_step = [project([packed, up[1], down[1]]), project([up[2], down[2]])]
    near = after(jnp.where(z % 2 == 0, down[1][:rows], up[1][:rows]), by_step[0])
    pair_rows = jnp.concatenate([image_rows, near], axis=0)
    hidden_in = jnp.concatenate([pair_rows, lax.ppermute(pair_rows, "y", swap)], axis=0)

    by_step.append(project([up[3], after(down[3], far), far]))
    offsets = [0, -1, 1, -2, 2, -3, 3, 4]
    text_parts = [packed] + [part for k in (1, 2, 3) for part in (up[k], down[k])] + [far]
    text_norm = modulate(jnp.concatenate([p[rows:] for p in text_parts], axis=0), mod[4], mod[3])
    text_kv = dot_t(text_t, text_norm).astype(BF16)
    text_kv = jnp.concatenate(
        [jnp.pad(part, ((HEAD, 0), (0, 0))) for part in (text_kv[: 2 * HEAD], text_kv[2 * HEAD :])]
    )
    all_qkv = jnp.concatenate([by_step[0], by_step[1], by_step[2], text_kv], axis=1)
    in_order = all_qkv
    for i, offset in enumerate(offsets[1:7]):
        piece = all_qkv[:, (i + 1) * rows : (i + 2) * rows]
        in_order = lax.dynamic_update_slice_in_dim(
            in_order, piece, (((z + offset) % 8) ^ z) * rows, 1
        )
    in_order = lax.dynamic_update_slice_in_dim(
        in_order, all_qkv[:, 7 * rows : 8 * rows], 4 * rows, 1
    )
    send = in_order[per_head:]
    got = lax.ppermute(send, "y", swap)
    mlp_packed = after(mlp_packed, send)
    mlp_fetched = [lax.ppermute(mlp_packed, "zb", xor_perm(4, m)) for m in (1, 2, 3)]


    z_of = (z + jnp.array(offsets, jnp.int32)) % 8
    slots = (z_of[None, :] * 2 + (y ^ jnp.arange(2))[:, None])[:, :, None] * text_own
    in_pad = jnp.arange(text_pad)
    text_valid = (slots + in_pad < text_lengths[0, 0]) & (in_pad < text_own)
    text_valid = text_valid.reshape(2, 8 * text_pad)
    image_total = 16 * rows
    always = jnp.ones((8 * rows,), bool)
    valid = jnp.concatenate([always, text_valid[0], always, text_valid[1]])

    mine = after(in_order[:per_head], hidden_in)
    keys = jnp.concatenate([mine[HEAD : 2 * HEAD], got[HEAD : 2 * HEAD]], axis=1)
    values = jnp.concatenate([mine[2 * HEAD :], got[2 * HEAD :]], axis=1)
    def attend(query_block):
        scores = (
            lax.dot_general(query_block, keys, (((0,), (0,)), ((), ())), preferred_element_type=F32)
            * HEAD**-0.5
        )
        scores = jnp.where(valid[None, :], scores, -1e30)
        row_max = jnp.max(scores, axis=1, keepdims=True)
        weights = jnp.exp(scores - row_max)
        total = jnp.sum(weights, axis=1)
        mixed = dot_t(values, weights.astype(BF16)) / total[None, :]
        return mixed.astype(BF16)

    pair = 2 * rows
    attended = [
        attend(
            jnp.concatenate([part[:HEAD, m * pair : (m + 1) * pair] for part in (mine, got)], axis=1)
        )
        for m in range(4)
    ]
    returned = jnp.concatenate(
        [attended[0]] + [lax.ppermute(attended[m], "zb", xor_perm(4, m)) for m in (1, 2, 3)], axis=0
    )
    groups = [xor_perm(4, (k & 1) * 2 + (k >> 1)) for k in range(4)]
    from_a = [returned] + [lax.ppermute(returned, A, groups[j]) for j in (1, 2, 3)]

    mlp_fetched = after(mlp_fetched, *attended)
    mlp_pieces = jnp.concatenate(
        [p.reshape(1, 2, unit_piece, width) for p in mlp_fetched], axis=0
    )
    left = lax.ppermute(mlp_pieces, "x", rot_perm(4, 1))
    right = lax.ppermute(mlp_pieces, "x", rot_perm(4, -1))
    left, right = after((left, right), *from_a)
    near_half = jnp.concatenate([mlp_pieces, left, right], axis=0)
    near_other = lax.ppermute(near_half, "core", swap)
    far_in = lax.ppermute(left[:, 0], "x", rot_perm(4, 1))
    far_out = lax.ppermute(right[:, 1], "x", rot_perm(4, -1))
    reordered = [
        jnp.concatenate([part[:, (j ^ k) * rows : ((j ^ k) + 1) * rows] for k in range(4)], axis=1)
        for j, part in enumerate(from_a)
    ]
    mlp_norm, inner_own, own_hidden = project_rows(
        z * 2 + y, jnp.concatenate(reordered, axis=0), hidden_in, mod, mlp_in_weight, proj_weight
    )
    far_in, far_out = after((far_in, far_out), mlp_norm)
    far_half = jnp.stack([far_in, far_out], axis=1)
    far_other = lax.ppermute(far_half, "core", swap)
    partial = mlp_rows(
        mlp_norm, inner_own, mlp_out_weight, [near_half, far_half, near_other, far_other]
    )
    mlp_out = partial[:rows].astype(F32)
    for k in (1, 2, 3):
        mlp_out = mlp_out + lax.ppermute(partial[k * rows : (k + 1) * rows], A, groups[k]).astype(F32)
    block_out = own_hidden + mod[9] * mlp_out
    final_norm = modulate(block_out, mod[6], mod[5])
    own_vel = dot_t(final_weight, final_norm)
    partner_vel = lax.ppermute(own_vel.astype(BF16), "cfg", xor_perm(2, 1)).astype(F32)
    leading = lax.axis_index("cfg") == 0
    cond_vel = jnp.where(leading, own_vel, partner_vel)
    uncond_vel = jnp.where(leading, partner_vel, own_vel)
    guided = uncond_vel + guidance[0] * (cond_vel - uncond_vel)
    first_row = lax.broadcasted_iota(jnp.int32, (16, 2, 128), 1) == 0
    sums = jnp.where(first_row, jnp.sum(cond_vel * cond_vel), jnp.sum(guided * guided))
    sums = lax.all_to_all(sums, SEQ, 0, 0, tiled=True)
    totals = jnp.sum(sums[:, :, 0], axis=0)
    entries = own_vel.shape[0] * image_total
    rms_cond = jnp.sqrt(totals[0] / entries + EPS_NORM)
    rms_guided = jnp.sqrt(totals[1] / entries + EPS_NORM)
    result_vel = 0.7 * (guided * (rms_cond / rms_guided)) + 0.3 * guided
    channel_half = latents.shape[1]
    own_channels = lax.dynamic_slice_in_dim(
        result_vel, lax.axis_index("cfg") * channel_half, channel_half, 0
    )
    next_index = jnp.minimum(step_index[0] + step_count[0], STEPS)
    step_size = sigma_of(next_index) - sigma_of(step_index[0])
    moved = latents[0] + step_size * own_channels
    return (own_channels[None], moved[None])


def solution(mesh):
    split = Mesh(mesh.devices.reshape(2, 4, 2, 4, 2, 2), ("cfg", "x", "core", "zb", "z0", "y"))
    req, seq = ("x", "core"), SEQ
    in_specs = (
        P("cfg", req, seq, None),
        P("cfg", req, seq, None),
        P("cfg", req, None, None),
        P(None, seq),
        P(),
        P(None, seq),
        P(seq, None),
        P(),
        P(req, "cfg", seq),
        P(req),
        P("cfg", req),
        P(req),
        P(req),
    )
    out_specs = (P(req, "cfg", seq), P(req, "cfg", seq))
    return jax.shard_map(local, mesh=split, in_specs=in_specs, out_specs=out_specs, check_vma=False)
```

```python
import jax
import jax.numpy as jnp
from jax import lax
from jax.experimental import pallas as pl
from jax.experimental.pallas import tpu as pltpu
from jax.sharding import Mesh, PartitionSpec as P

HEADS = 16
HEAD = 64
STEPS = 28
EPS_NORM = 1e-06
F32 = jnp.float32
BF16 = jnp.bfloat16
Z = ("zb", "z0")
A = ("z0", "y")
SEQ = ("zb", "z0", "y")
UNIT_PIECE = 48


def xor_perm(size, mask):
    return [(i, i ^ mask) for i in range(size)]


def rot_perm(size, step):
    return [(i, (i + step) % size) for i in range(size)]


def modulate(rows_in, scale_row, shift_row):
    values = rows_in.astype(F32)
    center = jnp.mean(values, axis=-1, keepdims=True)
    spread = jnp.mean(jnp.square(values - center), axis=-1, keepdims=True)
    return (
        (values - center) * lax.rsqrt(spread + EPS_NORM) * (1.0 + scale_row) + shift_row
    ).astype(BF16)


def sigma_of(index):
    remain = 1.0 - index.astype(F32) / STEPS
    return 3.0 * remain / (1.0 + 2.0 * remain)


def dot_t(left, right):
    return lax.dot_general(left, right, (((1,), (1,)), ((), ())), preferred_element_type=F32)


def norm_rows(values, scale_row, shift_row):
    center = jnp.mean(values, axis=-1, keepdims=True)
    spread = jnp.mean(jnp.square(values - center), axis=-1, keepdims=True)
    return (
        (values - center) * lax.rsqrt(spread + EPS_NORM) * (1.0 + scale_row) + shift_row
    ).astype(BF16)


def gelu(values):
    return 0.5 * values * (1.0 + jnp.tanh(0.7978845608028654 * (values + 0.044715 * values**3)))


def project_kernel(
    place_ref,
    attended_ref,
    hidden_in_ref,
    mod_ref,
    own_in_ref,
    proj_ref,
    norm_ref,
    inner_ref,
    hidden_ref,
    proj,
    mixed_rows,
    hidden,
    sems,
):
    place = place_ref[0]
    copies = []
    for j in range(4):
        for m in range(4):
            block = place ^ (4 * m + (j & 1) * 2 + (j >> 1))
            target = proj.at[pl.ds((4 * j + m) * HEAD, HEAD)]
            copies.append(pltpu.make_async_copy(proj_ref.at[block], target, sems.at[4 * j + m]))
            copies[-1].start()
    mixed_rows[...] = attended_ref[...].T
    for copy in copies:
        copy.wait()
    rows, width = norm_ref.shape
    tile = 384

    @pl.loop(0, width // tile)
    def _(i):
        cols = pl.ds(pl.multiple_of(i * tile, tile), tile)
        mixed = jnp.dot(mixed_rows[...], proj[:, cols], preferred_element_type=F32)
        hidden[:, cols] = hidden_in_ref[:, cols].astype(F32) + mod_ref[2:3, cols] * mixed

    hidden_ref[...] = hidden[: rows // 4]

    @pl.loop(0, rows // 64)
    def _(i):
        part = pl.ds(pl.multiple_of(i * 64, 64), 64)
        norm_ref[part, :] = norm_rows(hidden[part, :], mod_ref[8:9, :], mod_ref[7:8, :])

    inner_ref[...] = gelu(
        jnp.dot(norm_ref[...], own_in_ref[...], preferred_element_type=F32)
    ).astype(BF16)


def mlp_kernel(norm_ref, inner_own_ref, own_out_ref, *refs):
    pieces, (partial_ref, far_in, far_out, inner, sems) = refs[:4], refs[4:]
    copies = []
    base = 0
    for ref in pieces:
        count = ref.shape[0]
        for side, target in enumerate((far_in, far_out)):
            copies.append(
                pltpu.make_async_copy(
                    ref.at[:, side], target.at[pl.ds(base, count)], sems.at[len(copies)]
                )
            )
            copies[-1].start()
        base += count
    for copy in copies[::2]:
        copy.wait()
    width = partial_ref.shape[1]
    tile = 384
    group = tile // far_in.shape[1]

    @pl.loop(0, far_in.shape[0] // group)
    def _(i):
        part = far_in[pl.ds(i * group, group)].reshape(tile, width)
        inner[:, pl.ds(pl.multiple_of(i * tile, tile), tile)] = gelu(
            dot_t(norm_ref[...], part)
        ).astype(BF16)

    for copy in copies[1::2]:
        copy.wait()

    @pl.loop(0, width // tile)
    def _(i):
        cols = pl.ds(pl.multiple_of(i * tile, tile), tile)
        partial_ref[:, cols] = (
            jnp.dot(inner_own_ref[...], own_out_ref[:, cols], preferred_element_type=F32)
            + jnp.dot(
                inner[...], far_out[:, :, cols].reshape(-1, tile), preferred_element_type=F32
            )
        ).astype(BF16)


VMEM = pl.BlockSpec(memory_space=pltpu.VMEM)
ANYWHERE = pl.BlockSpec(memory_space=pl.ANY)


def project_rows(place, attended, hidden_in, mod, own_in, proj_weight):
    rows, width = hidden_in.shape
    units = own_in.shape[1]
    return pl.pallas_call(
        project_kernel,
        in_specs=[pl.BlockSpec(memory_space=pltpu.SMEM)] + [VMEM] * 4 + [ANYWHERE],
        out_specs=[VMEM] * 3,
        out_shape=[
            jax.ShapeDtypeStruct((rows, width), BF16),
            jax.ShapeDtypeStruct((rows, units), BF16),
            jax.ShapeDtypeStruct((rows // 4, width), F32),
        ],
        scratch_shapes=[
            pltpu.VMEM((HEADS * HEAD, width), BF16),
            pltpu.VMEM((rows, HEADS * HEAD), BF16),
            pltpu.VMEM((rows, width), F32),
            pltpu.SemaphoreType.DMA((HEADS,)),
        ],
        compiler_params=pltpu.CompilerParams(vmem_limit_bytes=32 * 2**20),
        cost_estimate=pl.CostEstimate(
            flops=2 * rows * width * (HEADS * HEAD + units),
            bytes_accessed=10 * 2**20,
            transcendentals=rows * units,
        ),
    )(place[None], attended, hidden_in, mod, own_in, proj_weight.reshape(HEADS, HEAD, width))


def mlp_rows(norm, inner_own, own_out, pieces):
    rows, width = norm.shape
    far = 3 * own_out.shape[0]
    return pl.pallas_call(
        mlp_kernel,
        in_specs=[VMEM] * 3 + [ANYWHERE] * 4,
        out_specs=VMEM,
        out_shape=jax.ShapeDtypeStruct((rows, width), BF16),
        scratch_shapes=[
            pltpu.VMEM((far // UNIT_PIECE, UNIT_PIECE, width), BF16),
            pltpu.VMEM((far // UNIT_PIECE, UNIT_PIECE, width), BF16),
            pltpu.VMEM((rows, far), BF16),
            pltpu.SemaphoreType.DMA((8,)),
        ],
        compiler_params=pltpu.CompilerParams(vmem_limit_bytes=32 * 2**20),
        cost_estimate=pl.CostEstimate(
            flops=4 * rows * width * far,
            bytes_accessed=12 * 2**20,
            transcendentals=rows * far,
        ),
    )(norm, inner_own, own_out, *pieces)


def after(value, *earlier):
    return lax.optimization_barrier((value, earlier))[0]


def local(
    image_hidden,
    text_hidden,
    modulation,
    attn_weight,
    proj_weight,
    mlp_in_weight,
    mlp_out_weight,
    final_weight,
    latents,
    guidance,
    text_lengths,
    step_index,
    step_count,
):
    image_rows = image_hidden[0, 0]
    text_rows = text_hidden[0, 0]
    mod = modulation[0, 0]
    rows = image_rows.shape[0]
    width = image_rows.shape[1]
    text_own = text_rows.shape[0]
    replica = lax.axis_index("x") * 2 + lax.axis_index("core")
    z, y = lax.axis_index(Z), lax.axis_index("y")
    ahead, back = rot_perm(8, 1), rot_perm(8, -1)
    swap = xor_perm(2, 1)

    text_pad = 16
    packed = jnp.concatenate(
        [image_rows, jnp.pad(text_rows, ((0, text_pad - text_own), (0, 0)))], axis=0
    )
    units = mlp_out_weight.shape[0]
    unit_piece = units // 8
    mlp_packed = jnp.concatenate(
        [
            lax.dynamic_slice_in_dim(mlp_in_weight, replica * unit_piece, unit_piece, 1).T,
            lax.dynamic_slice_in_dim(mlp_out_weight, replica * unit_piece, unit_piece, 0),
        ],
        axis=0,
    )
    up, down = [packed], [packed]
    for k in range(3):
        if k == 1:
            up[1], down[1] = after((up[1], down[1]), mlp_packed)
        up.append(lax.ppermute(up[-1], Z, ahead))
        down.append(lax.ppermute(down[-1], Z, back))
    cut = rows // 2
    far_low = lax.ppermute(up[3][:cut], Z, ahead)
    far_high = lax.ppermute(down[3][cut:], Z, back)
    far = jnp.concatenate([far_low, far_high], axis=0)
    other_weight = lax.ppermute(attn_weight, "y", swap)

    per_head = 3 * HEAD
    own_t, other_t = after((attn_weight, other_weight), up[1], down[1])
    own_t, other_t = own_t.T, other_t.T
    image_t = jnp.concatenate([own_t[:per_head], other_t[:per_head]], axis=0)
    text_t = jnp.concatenate([own_t[per_head:], other_t[per_head:]], axis=0)

    def project(parts):
        norm = modulate(jnp.concatenate([part[:rows] for part in parts], axis=0), mod[1], mod[0])
        return dot_t(image_t, norm).astype(BF16)

    by_step = [project([packed, up[1], down[1]]), project([up[2], down[2]])]
    near = after(jnp.where(z % 2 == 0, down[1][:rows], up[1][:rows]), by_step[0])
    pair_rows = jnp.concatenate([image_rows, near], axis=0)
    hidden_in = jnp.concatenate([pair_rows, lax.ppermute(pair_rows, "y", swap)], axis=0)

    by_step.append(project([up[3], after(down[3], far), far]))
    offsets = [0, -1, 1, -2, 2, -3, 3, 4]
    text_parts = [packed] + [part for k in (1, 2, 3) for part in (up[k], down[k])] + [far]
    text_norm = modulate(jnp.concatenate([p[rows:] for p in text_parts], axis=0), mod[4], mod[3])
    text_kv = dot_t(text_t, text_norm).astype(BF16)
    text_kv = jnp.concatenate(
        [jnp.pad(part, ((HEAD, 0), (0, 0))) for part in (text_kv[: 2 * HEAD], text_kv[2 * HEAD :])]
    )
    all_qkv = jnp.concatenate([by_step[0], by_step[1], by_step[2], text_kv], axis=1)
    in_order = all_qkv
    for i, offset in enumerate(offsets[1:7]):
        piece = all_qkv[:, (i + 1) * rows : (i + 2) * rows]
        in_order = lax.dynamic_update_slice_in_dim(
            in_order, piece, (((z + offset) % 8) ^ z) * rows, 1
        )
    in_order = lax.dynamic_update_slice_in_dim(
        in_order, all_qkv[:, 7 * rows : 8 * rows], 4 * rows, 1
    )
    send = in_order[per_head:]
    got = lax.ppermute(send, "y", swap)
    mlp_packed = after(mlp_packed, send)
    mlp_fetched = [lax.ppermute(mlp_packed, "zb", xor_perm(4, m)) for m in (1, 2, 3)]


    z_of = (z + jnp.array(offsets, jnp.int32)) % 8
    slots = (z_of[None, :] * 2 + (y ^ jnp.arange(2))[:, None])[:, :, None] * text_own
    in_pad = jnp.arange(text_pad)
    text_valid = (slots + in_pad < text_lengths[0, 0]) & (in_pad < text_own)
    text_valid = text_valid.reshape(2, 8 * text_pad)
    image_total = 16 * rows
    always = jnp.ones((8 * rows,), bool)
    valid = jnp.concatenate([always, text_valid[0], always, text_valid[1]])

    mine = after(in_order[:per_head], hidden_in)
    keys = jnp.concatenate([mine[HEAD : 2 * HEAD], got[HEAD : 2 * HEAD]], axis=1)
    values = jnp.concatenate([mine[2 * HEAD :], got[2 * HEAD :]], axis=1)
    def attend(query_block):
        scores = (
            lax.dot_general(query_block, keys, (((0,), (0,)), ((), ())), preferred_element_type=F32)
            * HEAD**-0.5
        )
        scores = jnp.where(valid[None, :], scores, -1e30)
        row_max = jnp.max(scores, axis=1, keepdims=True)
        weights = jnp.exp(scores - row_max)
        total = jnp.sum(weights, axis=1)
        mixed = dot_t(values, weights.astype(BF16)) / total[None, :]
        return mixed.astype(BF16)

    pair = 2 * rows
    attended = [
        attend(
            jnp.concatenate([part[:HEAD, m * pair : (m + 1) * pair] for part in (mine, got)], axis=1)
        )
        for m in range(4)
    ]
    returned = jnp.concatenate(
        [attended[0]] + [lax.ppermute(attended[m], "zb", xor_perm(4, m)) for m in (1, 2, 3)], axis=0
    )
    groups = [xor_perm(4, (k & 1) * 2 + (k >> 1)) for k in range(4)]
    from_a = [returned] + [lax.ppermute(returned, A, groups[j]) for j in (1, 2, 3)]

    mlp_fetched = after(mlp_fetched, *attended)
    mlp_pieces = jnp.concatenate(
        [p.reshape(1, 2, unit_piece, width) for p in mlp_fetched], axis=0
    )
    left = lax.ppermute(mlp_pieces, "x", rot_perm(4, 1))
    right = lax.ppermute(mlp_pieces, "x", rot_perm(4, -1))
    left, right = after((left, right), from_a[1], from_a[3])
    near_half = jnp.concatenate([mlp_pieces, left, right], axis=0)
    near_other = lax.ppermute(near_half, "core", swap)
    far_in = lax.ppermute(left[:, 0], "x", rot_perm(4, 1))
    far_out = lax.ppermute(right[:, 1], "x", rot_perm(4, -1))
    reordered = [
        jnp.concatenate([part[:, (j ^ k) * rows : ((j ^ k) + 1) * rows] for k in range(4)], axis=1)
        for j, part in enumerate(from_a)
    ]
    mlp_norm, inner_own, own_hidden = project_rows(
        z * 2 + y, jnp.concatenate(reordered, axis=0), hidden_in, mod, mlp_in_weight, proj_weight
    )
    far_in, far_out = after((far_in, far_out), mlp_norm)
    far_half = jnp.stack([far_in, far_out], axis=1)
    far_other = lax.ppermute(far_half, "core", swap)
    partial = mlp_rows(
        mlp_norm, inner_own, mlp_out_weight, [near_half, far_half, near_other, far_other]
    )
    mlp_out = partial[:rows].astype(F32)
    for k in (1, 2, 3):
        mlp_out = mlp_out + lax.ppermute(partial[k * rows : (k + 1) * rows], A, groups[k]).astype(F32)
    block_out = own_hidden + mod[9] * mlp_out
    final_norm = modulate(block_out, mod[6], mod[5])
    own_vel = dot_t(final_weight, final_norm)
    partner_vel = lax.ppermute(own_vel.astype(BF16), "cfg", xor_perm(2, 1)).astype(F32)
    leading = lax.axis_index("cfg") == 0
    cond_vel = jnp.where(leading, own_vel, partner_vel)
    uncond_vel = jnp.where(leading, partner_vel, own_vel)
    guided = uncond_vel + guidance[0] * (cond_vel - uncond_vel)
    first_half = lax.broadcasted_iota(jnp.int32, (16, 1, 128), 2) < 64
    sums = jnp.where(first_half, jnp.sum(cond_vel * cond_vel), jnp.sum(guided * guided))
    sums = lax.all_to_all(sums, SEQ, 0, 0, tiled=True)
    totals = jnp.sum(sums[:, 0], axis=0)[::64]
    entries = own_vel.shape[0] * image_total
    rms_cond = jnp.sqrt(totals[0] / entries + EPS_NORM)
    rms_guided = jnp.sqrt(totals[1] / entries + EPS_NORM)
    result_vel = 0.7 * (guided * (rms_cond / rms_guided)) + 0.3 * guided
    channel_half = latents.shape[1]
    own_channels = lax.dynamic_slice_in_dim(
        result_vel, lax.axis_index("cfg") * channel_half, channel_half, 0
    )
    next_index = jnp.minimum(step_index[0] + step_count[0], STEPS)
    step_size = sigma_of(next_index) - sigma_of(step_index[0])
    moved = latents[0] + step_size * own_channels
    return (own_channels[None], moved[None])


def solution(mesh):
    split = Mesh(mesh.devices.reshape(2, 4, 2, 4, 2, 2), ("cfg", "x", "core", "zb", "z0", "y"))
    req, seq = ("x", "core"), SEQ
    in_specs = (
        P("cfg", req, seq, None),
        P("cfg", req, seq, None),
        P("cfg", req, None, None),
        P(None, seq),
        P(),
        P(None, seq),
        P(seq, None),
        P(),
        P(req, "cfg", seq),
        P(req),
        P("cfg", req),
        P(req),
        P(req),
    )
    out_specs = (P(req, "cfg", seq), P(req, "cfg", seq))
    return jax.shard_map(local, mesh=split, in_specs=in_specs, out_specs=out_specs, check_vma=False)
```
